128 devices in a mesh: layer: 16 (over y, x), ex: 8 (over z, core).
Axes of the slice: x: 4, y: 4, z: 4, core: 2. Of those that a mesh axis runs over, the one named last changes fastest.
Arguments:
- partials: bfloat16 [16, 8192, 2048], P('layer', None, 'ex'), may hold values from -6 to 6
- scales: float32 [16, 128, 2048], P('layer', None, 'ex'), may hold values from 0.01 to 3.6, as said below
- pairs: int32 [80, 3], replicated, may hold values from 0 to 15, as said below
Outputs:
- gram: float32 [2048, 1280], P('ex')
The draws below stay inside these ranges and needn't reach their ends.
Inputs may be any that keep to these rules, and one draw needn't show every extreme that they name: Positive scales. `pairs`: each row is (row block, column block, computing index along ex, from 0 to 7). Block x is held by ex index x // 2. Rows s * 8 to (s + 1) * 8 - 1 name every block exactly once, and no row names one block twice. At most 20 rows name one computing index, and one index has exactly 20.
All inputs are finite; a program needn't handle non-finite values.
Results may differ from the reference program's by a relative error of at most 0.0041.
Values may be sent and summed in bfloat16 or wider, within the bound.
No kernel may reach another device: no remote copies, remote signals or barrier semaphores. Data moves between devices by JAX's collectives and lax.ppermute only.
A program may use at most 64 MiB of HBM per device.

```python
import math
import jax
import jax.numpy as jnp
from jax import lax

K = 8192
TB = 128
QB = 64
SLOTS = 10
LAYERS = 16
NB = 16
E = 2048
NPAIRS = 80
MAXP = 20
N_EX = 8


def draw_scales(key, part):
    row_scale = jnp.exp(jax.random.uniform(jax.random.fold_in(key, 1), (E,), jnp.float32, 0.0, math.log(10.0)))
    position = jnp.arange(K // QB, dtype=jnp.float32) / max(K // QB - 1, 1)
    ramp = jnp.exp(position * math.log(3.0))
    noise = jnp.exp(jax.random.uniform(jax.random.fold_in(key, 2), (LAYERS, K // QB, E), jnp.float32, math.log(0.5), math.log(2.0)))
    return 0.02 * noise * ramp[None, :, None] * row_scale[None, None, :]


def draw_pairs(key, part):
    rows_list = []
    cols_list = []
    for group_index in range(SLOTS):
        shuffled = jax.random.permutation(jax.random.fold_in(key, 10 + group_index), NB).astype(jnp.int32)
        rows_list.append(shuffled[0::2])
        cols_list.append(shuffled[1::2])
    row_block = jnp.concatenate(rows_list)
    col_block = jnp.concatenate(cols_list)
    positions = jax.random.permutation(jax.random.fold_in(key, 3), NPAIRS).astype(jnp.int32)
    busiest = jax.random.randint(jax.random.fold_in(key, 4), (), 0, N_EX).astype(jnp.int32)
    spread = (busiest + 1 + jnp.maximum(positions - MAXP, 0) % (N_EX - 1)) % N_EX
    computer = jnp.where(positions < MAXP, busiest, spread).astype(jnp.int32)
    return jnp.stack([row_block, col_block, computer], axis=1)


def level_of(key, shape, cuts, smallest, high):
    def one(dim, shards_of):
        steps = jax.random.uniform(jax.random.fold_in(jax.random.fold_in(key, 6), dim), (shards_of,), jnp.float32, smallest / len(cuts), high / len(cuts))
        return jnp.repeat(jnp.exp(steps), shape[dim] // shards_of).reshape((-1,) + (1,) * (len(shape) - dim - 1))

    factor_of = one(*cuts[0])
    for cut in cuts[1:]:
        factor_of = factor_of * one(*cut)
    return factor_of


def centred(rng, shape, width, limit, cuts=(), kind=jnp.bfloat16):
    entries = width * jax.random.normal(rng, shape, jnp.float32)
    if cuts:
        entries = entries * level_of(rng, shape, cuts, -0.22, 0.18)
    return jnp.clip(entries, -limit, limit).astype(kind)


def setup_inputs(seed: int = 0) -> dict:
    key_list = jax.random.split(jax.random.key(seed), 4)
    return {
        "partials": centred(key_list[0], (LAYERS, K, E), 1.0, 6.0, ((0, 16), (2, 8))),
        "scales": draw_scales(jax.random.fold_in(key_list[3], 71), 0),
        "pairs": draw_pairs(jax.random.fold_in(key_list[3], 71), 0),
    }


def reference(partials, scales, pairs):

    def add_layer(total, layer_data):
        piece_vals, scale_rows = layer_data
        dequant = piece_vals.astype(jnp.float32).reshape(K // QB, QB, E) * scale_rows[:, None, :]
        return (total + dequant.reshape(K, E), None)
    summed, _ = lax.scan(add_layer, jnp.zeros((K, E), jnp.float32), (partials, scales))
    mean_square = lax.optimization_barrier(jnp.mean(summed * summed, axis=0))
    unit_rows = (summed * lax.rsqrt(mean_square + 1e-06)).astype(jnp.bfloat16)
    by_block = unit_rows.reshape(K, NB, TB)
    per_group = NB // 2

    def one_block(block_index):
        own_rows = lax.dynamic_index_in_dim(by_block, block_index, axis=1, keepdims=False)
        pieces = []
        for group_index in range(SLOTS):
            grouped = pairs[group_index * per_group:(group_index + 1) * per_group]
            is_row = (grouped[:, 0] == block_index).astype(jnp.int32)
            is_col = (grouped[:, 1] == block_index).astype(jnp.int32)
            partner = jnp.sum(is_row * grouped[:, 1] + is_col * grouped[:, 0]).astype(jnp.int32)
            other_rows = lax.dynamic_index_in_dim(by_block, partner, axis=1, keepdims=False)
            tile_value = jnp.dot(own_rows.T, other_rows, preferred_element_type=jnp.float32)
            pieces.append(tile_value / math.sqrt(K))
        return jnp.concatenate(pieces, axis=1)
    gram = lax.map(one_block, jnp.arange(NB, dtype=jnp.int32))
    return gram.reshape(E, SLOTS * TB)
```

```python
import math

import jax
import jax.numpy as jnp
from jax import lax
from jax.experimental import pallas as pl
from jax.experimental.pallas import tpu as pltpu
from jax.sharding import PartitionSpec as P

K = 8192
TB = 128
QB = 64
SLOTS = 10
LAYERS = 16
N_EX = 8
BLK_DEV = 2
COLS = BLK_DEV * TB
SLICE = K // LAYERS
SCALES = SLICE // QB
ROWS = COLS // LAYERS
WIDE = SLOTS * TB
AUX = 2 * TB
OWN = SLOTS
BF, F32 = jnp.bfloat16, jnp.float32


def sum_layers(piece_ref, scale_ref, high_ref, low_ref):
    row = pl.program_id(0)
    total = None
    for layer in range(LAYERS):
        term = piece_ref[layer].astype(F32) * scale_ref[layer, pl.ds(row, 1), :]
        total = term if total is None else total + term
    high = total.astype(BF)
    high_ref[...] = high
    low_ref[...] = (total - high.astype(F32)).astype(BF)


def summed_slice(pieces, scales):
    block = pl.BlockSpec((QB, COLS), lambda i: (i, 0))
    return pl.pallas_call(
        sum_layers,
        grid=(SCALES,),
        in_specs=[
            pl.BlockSpec((LAYERS, QB, COLS), lambda i: (0, i, 0)),
            pl.BlockSpec((LAYERS, SCALES, COLS), lambda i: (0, 0, 0)),
        ],
        out_specs=[block, block],
        out_shape=[jax.ShapeDtypeStruct((SLICE, COLS), BF)] * 2,
        cost_estimate=pl.CostEstimate(
            flops=2 * LAYERS * SLICE * COLS,
            bytes_accessed=2 * LAYERS * SLICE * COLS,
            transcendentals=0,
        ),
    )(pieces, scales)


def tiles(where_ref, high_ref, low_ref, *refs):
    parts, (out_ref, dots, squares) = refs[:7], refs[7:]
    contract = (((0,), (0,)), ((), ()))
    high, low = high_ref[...], low_ref[...]
    for n, ref in enumerate((high_ref, *parts)):
        part = ref[...]
        dot = lax.dot_general(high, part, contract, preferred_element_type=F32)
        dot += lax.dot_general(low, part, contract, preferred_element_type=F32)
        wide = part.astype(F32)
        square = jnp.sum(wide * wide, axis=0, keepdims=True)
        for half in range(BLK_DEV):
            cut = slice(half * TB, (half + 1) * TB)
            dots[n * BLK_DEV + half] = dot[:, cut]
            squares[n * BLK_DEV + half] = jnp.broadcast_to(square[:, cut], (8, TB))
    exact = high.astype(F32) + low.astype(F32)
    own = jnp.sum(exact * exact, axis=0, keepdims=True)
    for b in range(BLK_DEV):
        rows = slice(b * TB, (b + 1) * TB)
        aux = []
        for s in range(SLOTS):
            at = where_ref[b * SLOTS + s]
            out_ref[rows, s * TB : (s + 1) * TB] = dots[at, rows, :].astype(BF)
            aux.append(squares[at][:1])
        aux.append(own[:, rows])
        aux.append(jnp.zeros((ROWS - SLOTS - 1, TB), F32))
        aux = jnp.concatenate(aux, axis=0)
        first = aux.astype(BF)
        second = (aux - first.astype(F32)).astype(BF)
        both = jnp.concatenate([first, second], axis=1)
        for i in range(TB // ROWS):
            out_ref[b * TB + i * ROWS : b * TB + (i + 1) * ROWS, WIDE:] = both


def partial_tiles(where, high, low, parts):
    return pl.pallas_call(
        tiles,
        in_specs=[pl.BlockSpec(memory_space=pltpu.SMEM)]
        + [pl.BlockSpec(memory_space=pltpu.VMEM)] * 9,
        out_specs=pl.BlockSpec(memory_space=pltpu.VMEM),
        out_shape=jax.ShapeDtypeStruct((COLS, WIDE + AUX), BF),
        scratch_shapes=[
            pltpu.VMEM((N_EX * BLK_DEV, COLS, TB), F32),
            pltpu.VMEM((N_EX * BLK_DEV, 8, TB), F32),
        ],
        compiler_params=pltpu.CompilerParams(vmem_limit_bytes=32 * 2**20),
        cost_estimate=pl.CostEstimate(
            flops=4 * SLICE * COLS * COLS * N_EX,
            bytes_accessed=2 * SLICE * COLS * 9 + 2 * COLS * (WIDE + AUX),
            transcendentals=0,
        ),
    )(where, high, low, *parts)


def finish(me_ref, sums_ref, out_ref):
    total = sums_ref[0].astype(F32)
    for layer in range(1, LAYERS):
        total += sums_ref[layer].astype(F32)
    squares = total[:, WIDE : WIDE + TB] + total[:, WIDE + TB :]
    inverse = lax.rsqrt(squares / K + 1e-06)
    first = lax.rem(me_ref[0], TB // ROWS) * ROWS
    lane = lax.broadcasted_iota(jnp.int32, (ROWS, TB), 1)
    row = lax.broadcasted_iota(jnp.int32, (ROWS, TB), 0)
    own = jnp.broadcast_to(inverse[OWN : OWN + 1], (ROWS, TB))
    left = jnp.sum(jnp.where(lane == first + row, own, 0.0), axis=1, keepdims=True)
    left = left / math.sqrt(K)
    for s in range(SLOTS):
        cut = slice(s * TB, (s + 1) * TB)
        value = (total[:, cut] * left * inverse[s : s + 1]).astype(BF)
        for layer in range(LAYERS):
            out_ref[layer, :, cut] = value


def finished_rows(me, sums):
    return pl.pallas_call(
        finish,
        in_specs=[
            pl.BlockSpec(memory_space=pltpu.SMEM),
            pl.BlockSpec(memory_space=pltpu.VMEM),
        ],
        out_specs=pl.BlockSpec(memory_space=pltpu.VMEM),
        out_shape=jax.ShapeDtypeStruct((LAYERS, ROWS, WIDE), BF),
        compiler_params=pltpu.CompilerParams(vmem_limit_bytes=32 * 2**20),
        cost_estimate=pl.CostEstimate(
            flops=LAYERS * ROWS * WIDE,
            bytes_accessed=4 * LAYERS * ROWS * WIDE,
            transcendentals=ROWS * TB,
        ),
    )(me, sums)


def partner_places(pairs, ex):
    own = ex * BLK_DEV + jnp.arange(BLK_DEV, dtype=jnp.int32)[:, None, None]
    grouped = pairs.reshape(1, SLOTS, -1, 3)
    row, col = grouped[..., 0], grouped[..., 1]
    partner = jnp.sum(
        jnp.where(row == own, col, 0) + jnp.where(col == own, row, 0), axis=2
    )
    holder, half = partner // BLK_DEV, partner % BLK_DEV
    turn = (ex // 2 - holder // 2) % (N_EX // 2)
    other = (holder % 2) != (ex % 2)
    part = turn + jnp.where(other, N_EX // 2, 0)
    return (part * BLK_DEV + half).reshape(-1).astype(jnp.int32)


def on_device(partials, scales, pairs):
    ex = lax.axis_index("ex")
    here = lax.axis_index("layer").astype(jnp.int32).reshape(1)
    where = partner_places(pairs, ex)
    across = lambda a: lax.all_to_all(a, "layer", 0, 0, tiled=True)
    slice_scales = across(scales.reshape(LAYERS, SCALES, COLS))
    pieces = across(partials.reshape(LAYERS, SLICE, COLS))
    high, low = summed_slice(pieces, slice_scales)

    around = lambda a, d: lax.ppermute(
        a, "ex", [(e, (e + 2 * d) % N_EX) for e in range(N_EX)]
    )
    swap = lambda a: lax.ppermute(a, "ex", [(e, e ^ 1) for e in range(N_EX)])
    same = [around(high, d) for d in (1, 2, 3)]
    other = [swap(a) for a in (high, *same)]
    sums = partial_tiles(where, high, low, (*same, *other))

    sums = across(sums.reshape(LAYERS, ROWS, WIDE + AUX))
    rows = across(finished_rows(here, sums))
    return rows.reshape(COLS, WIDE).astype(F32)


def solution(mesh):
    in_specs = (P("layer", None, "ex"), P("layer", None, "ex"), P())
    out_specs = P("ex", None)
    return jax.shard_map(
        on_device, mesh=mesh, in_specs=in_specs, out_specs=out_specs, check_vma=False
    )
```

```python
import math

import jax
import jax.numpy as jnp
from jax import lax
from jax.experimental import pallas as pl
from jax.experimental.pallas import tpu as pltpu
from jax.sharding import PartitionSpec as P

K = 8192
TB = 128
QB = 64
SLOTS = 10
LAYERS = 16
N_EX = 8
BLK_DEV = 2
COLS = BLK_DEV * TB
SLICE = K // LAYERS
SIDE = 4
PART = K // 2 // SIDE
PART_SCALES = PART // QB
QUARTER = PART // SIDE
ROWS = COLS // LAYERS
WIDE = SLOTS * TB
AUX = 2 * TB
OWN = SLOTS
BF, F32 = jnp.bfloat16, jnp.float32


def lay_out(place_ref, piece_ref, scale_ref, *refs):
    outs, sem = refs[:-1], refs[-1]
    copies = []
    for half in range(2):
        for turn in range(SIDE):
            n = half * SIDE + turn
            part = lax.rem(place_ref[1 - half] + turn, SIDE)
            first = pl.multiple_of(half * (K // 2) + part * PART, PART)
            copy = pltpu.make_async_copy(
                piece_ref.at[pl.ds(first, PART)], outs[n].at[:PART], sem.at[n]
            )
            copy.start()
            copies.append(copy)
    for half in range(2):
        for turn in range(SIDE):
            part = lax.rem(place_ref[1 - half] + turn, SIDE)
            first = half * (K // 2 // QB) + part * PART_SCALES
            first = pl.multiple_of(first, PART_SCALES)
            scale = scale_ref[pl.ds(first, PART_SCALES), :]
            high = scale.astype(BF)
            outs[half * SIDE + turn][PART:, :] = jnp.concatenate(
                [high, (scale - high.astype(F32)).astype(BF)], axis=0
            )
    for copy in copies:
        copy.wait()


def laid_out(place, pieces, scales):
    shape = jax.ShapeDtypeStruct((PART + 2 * PART_SCALES, COLS), BF)
    return pl.pallas_call(
        lay_out,
        in_specs=[
            pl.BlockSpec(memory_space=pltpu.SMEM),
            pl.BlockSpec(memory_space=pltpu.HBM),
            pl.BlockSpec(memory_space=pltpu.VMEM),
        ],
        out_specs=[pl.BlockSpec(memory_space=pltpu.VMEM)] * (2 * SIDE),
        out_shape=[shape] * (2 * SIDE),
        scratch_shapes=[pltpu.SemaphoreType.DMA((2 * SIDE,))],
        compiler_params=pltpu.CompilerParams(vmem_limit_bytes=32 * 2**20),
        cost_estimate=pl.CostEstimate(
            flops=0, bytes_accessed=4 * K * COLS, transcendentals=0
        ),
    )(place, pieces, scales)


def sum_first(place_ref, *refs):
    pieces, outs, scales = refs[: 2 * SIDE], refs[2 * SIDE : -1], refs[-1]
    for n, ref in enumerate(pieces):
        both = ref[PART:, :].astype(F32)
        scales[n] = both[:PART_SCALES] + both[PART_SCALES:]
    for half in range(2):
        for turn in range(SIDE):
            part = lax.rem(place_ref[half] + turn, SIDE)
            for block in range(QUARTER // QB):
                row = part * (QUARTER // QB) + block
                first = pl.multiple_of(row * QB, QB)
                total = None
                for n in range(half * SIDE, (half + 1) * SIDE):
                    term = pieces[n][pl.ds(first, QB), :].astype(F32)
                    term = term * scales[n, pl.ds(row, 1), :]
                    total = term if total is None else total + term
                out = outs[half * SIDE + turn]
                out[block * QB : (block + 1) * QB, :] = total


def summed_first(place, pieces):
    return pl.pallas_call(
        sum_first,
        in_specs=[pl.BlockSpec(memory_space=pltpu.SMEM)]
        + [pl.BlockSpec(memory_space=pltpu.VMEM)] * (2 * SIDE),
        out_specs=[pl.BlockSpec(memory_space=pltpu.VMEM)] * (2 * SIDE),
        out_shape=[jax.ShapeDtypeStruct((QUARTER, COLS), F32)] * (2 * SIDE),
        scratch_shapes=[pltpu.VMEM((2 * SIDE, PART_SCALES, COLS), F32)],
        compiler_params=pltpu.CompilerParams(vmem_limit_bytes=32 * 2**20),
        cost_estimate=pl.CostEstimate(
            flops=2 * K * COLS, bytes_accessed=4 * K * COLS, transcendentals=0
        ),
    )(place, *pieces)


def sum_second(*refs):
    pieces, (high_ref, low_ref) = refs[: 2 * SIDE], refs[2 * SIDE :]
    for half in range(2):
        total = pieces[half * SIDE][...]
        for n in range(half * SIDE + 1, (half + 1) * SIDE):
            total += pieces[n][...]
        high = total.astype(BF)
        rows = slice(half * QUARTER, (half + 1) * QUARTER)
        high_ref[rows, :] = high
        low_ref[rows, :] = (total - high.astype(F32)).astype(BF)


def summed_second(pieces):
    return pl.pallas_call(
        sum_second,
        in_specs=[pl.BlockSpec(memory_space=pltpu.VMEM)] * (2 * SIDE),
        out_specs=[pl.BlockSpec(memory_space=pltpu.VMEM)] * 2,
        out_shape=[jax.ShapeDtypeStruct((SLICE, COLS), BF)] * 2,
        compiler_params=pltpu.CompilerParams(vmem_limit_bytes=32 * 2**20),
        cost_estimate=pl.CostEstimate(
            flops=8 * SLICE * COLS, bytes_accessed=20 * SLICE * COLS, transcendentals=0
        ),
    )(*pieces)


def tiles(where_ref, high_ref, low_ref, *refs):
    parts, (out_ref, dots, squares) = refs[:7], refs[7:]
    contract = (((0,), (0,)), ((), ()))
    high, low = high_ref[...], low_ref[...]
    for n, ref in enumerate((high_ref, *parts)):
        part = ref[...]
        dot = lax.dot_general(high, part, contract, preferred_element_type=F32)
        dot += lax.dot_general(low, part, contract, preferred_element_type=F32)
        wide = part.astype(F32)
        square = jnp.sum(wide * wide, axis=0, keepdims=True)
        for half in range(BLK_DEV):
            cut = slice(half * TB, (half + 1) * TB)
            dots[n * BLK_DEV + half] = dot[:, cut]
            squares[n * BLK_DEV + half] = jnp.broadcast_to(square[:, cut], (8, TB))
    exact = high.astype(F32) + low.astype(F32)
    own = jnp.sum(exact * exact, axis=0, keepdims=True)
    for b in range(BLK_DEV):
        rows = slice(b * TB, (b + 1) * TB)
        aux = []
        for s in range(SLOTS):
            at = where_ref[b * SLOTS + s]
            out_ref[rows, s * TB : (s + 1) * TB] = dots[at, rows, :].astype(BF)
            aux.append(squares[at][:1])
        aux.append(own[:, rows])
        aux.append(jnp.zeros((ROWS - SLOTS - 1, TB), F32))
        aux = jnp.concatenate(aux, axis=0)
        first = aux.astype(BF)
        second = (aux - first.astype(F32)).astype(BF)
        both = jnp.concatenate([first, second], axis=1)
        for i in range(TB // ROWS):
            out_ref[b * TB + i * ROWS : b * TB + (i + 1) * ROWS, WIDE:] = both


def partial_tiles(where, high, low, parts):
    return pl.pallas_call(
        tiles,
        in_specs=[pl.BlockSpec(memory_space=pltpu.SMEM)]
        + [pl.BlockSpec(memory_space=pltpu.VMEM)] * 9,
        out_specs=pl.BlockSpec(memory_space=pltpu.VMEM),
        out_shape=jax.ShapeDtypeStruct((COLS, WIDE + AUX), BF),
        scratch_shapes=[
            pltpu.VMEM((N_EX * BLK_DEV, COLS, TB), F32),
            pltpu.VMEM((N_EX * BLK_DEV, 8, TB), F32),
        ],
        compiler_params=pltpu.CompilerParams(vmem_limit_bytes=32 * 2**20),
        cost_estimate=pl.CostEstimate(
            flops=4 * SLICE * COLS * COLS * N_EX,
            bytes_accessed=2 * SLICE * COLS * 9 + 2 * COLS * (WIDE + AUX),
            transcendentals=0,
        ),
    )(where, high, low, *parts)


def finish(me_ref, sums_ref, out_ref):
    total = sums_ref[0].astype(F32)
    for layer in range(1, LAYERS):
        total += sums_ref[layer].astype(F32)
    squares = total[:, WIDE : WIDE + TB] + total[:, WIDE + TB :]
    inverse = lax.rsqrt(squares / K + 1e-06)
    first = lax.rem(me_ref[0], TB // ROWS) * ROWS
    lane = lax.broadcasted_iota(jnp.int32, (ROWS, TB), 1)
    row = lax.broadcasted_iota(jnp.int32, (ROWS, TB), 0)
    own = jnp.broadcast_to(inverse[OWN : OWN + 1], (ROWS, TB))
    left = jnp.sum(jnp.where(lane == first + row, own, 0.0), axis=1, keepdims=True)
    left = left / math.sqrt(K)
    for s in range(SLOTS):
        cut = slice(s * TB, (s + 1) * TB)
        value = (total[:, cut] * left * inverse[s : s + 1]).astype(BF)
        for layer in range(LAYERS):
            out_ref[layer, :, cut] = value


def finished_rows(me, sums):
    return pl.pallas_call(
        finish,
        in_specs=[
            pl.BlockSpec(memory_space=pltpu.SMEM),
            pl.BlockSpec(memory_space=pltpu.VMEM),
        ],
        out_specs=pl.BlockSpec(memory_space=pltpu.VMEM),
        out_shape=jax.ShapeDtypeStruct((LAYERS, ROWS, WIDE), BF),
        compiler_params=pltpu.CompilerParams(vmem_limit_bytes=32 * 2**20),
        cost_estimate=pl.CostEstimate(
            flops=LAYERS * ROWS * WIDE,
            bytes_accessed=4 * LAYERS * ROWS * WIDE,
            transcendentals=ROWS * TB,
        ),
    )(me, sums)


def partner_places(pairs, ex):
    own = ex * BLK_DEV + jnp.arange(BLK_DEV, dtype=jnp.int32)[:, None, None]
    grouped = pairs.reshape(1, SLOTS, -1, 3)
    row, col = grouped[..., 0], grouped[..., 1]
    partner = jnp.sum(
        jnp.where(row == own, col, 0) + jnp.where(col == own, row, 0), axis=2
    )
    holder, half = partner // BLK_DEV, partner % BLK_DEV
    turn = (ex // 2 - holder // 2) % (N_EX // 2)
    other = (holder % 2) != (ex % 2)
    part = turn + jnp.where(other, N_EX // 2, 0)
    return (part * BLK_DEV + half).reshape(-1).astype(jnp.int32)


def on_device(partials, scales, pairs):
    ex = lax.axis_index("ex")
    layer = lax.axis_index("layer").astype(jnp.int32)
    here = layer.reshape(1)
    place = jnp.stack([layer // SIDE, layer % SIDE])
    where = partner_places(pairs, ex)

    def along(axis, a, turn):
        go = lambda y, x: ((y + turn) % SIDE, x) if axis == 0 else (y, (x + turn) % SIDE)
        to = [go(n // SIDE, n % SIDE) for n in range(LAYERS)]
        return lax.ppermute(a, "layer", [(n, y * SIDE + x) for n, (y, x) in enumerate(to)])

    def exchanged(parts, axes):
        return [
            a if n % SIDE == 0 else along(axes[n // SIDE], a, n % SIDE)
            for n, a in enumerate(parts)
        ]

    parts = laid_out(place, partials[0], scales[0])
    parts = summed_first(place, exchanged(parts, (1, 0)))
    high, low = summed_second(exchanged(parts, (0, 1)))

    around = lambda a, d: lax.ppermute(
        a, "ex", [(e, (e + 2 * d) % N_EX) for e in range(N_EX)]
    )
    swap = lambda a: lax.ppermute(a, "ex", [(e, e ^ 1) for e in range(N_EX)])
    same = [around(high, d) for d in (1, 2, 3)]
    other = [swap(a) for a in (high, *same)]
    sums = partial_tiles(where, high, low, (*same, *other))

    across = lambda a: lax.all_to_all(a, "layer", 0, 0, tiled=True)
    sums = across(sums.reshape(LAYERS, ROWS, WIDE + AUX))
    rows = across(finished_rows(here, sums))
    return rows.reshape(COLS, WIDE).astype(F32)


def solution(mesh):
    in_specs = (P("layer", None, "ex"), P("layer", None, "ex"), P())
    out_specs = P("ex", None)
    return jax.shard_map(
        on_device, mesh=mesh, in_specs=in_specs, out_specs=out_specs, check_vma=False
    )
```

```python
import functools
import math

import jax
import jax.numpy as jnp
from jax import lax
from jax.experimental import pallas as pl
from jax.experimental.pallas import tpu as pltpu
from jax.sharding import PartitionSpec as P

K = 8192
TB = 128
QB = 64
SLOTS = 10
LAYERS = 16
N_EX = 8
BLK_DEV = 2
COLS = BLK_DEV * TB
SLICE = K // LAYERS
SIDE = 4
PART = K // 2 // SIDE
PART_SCALES = PART // QB
QUARTER = PART // SIDE
ROWS = COLS // LAYERS
WIDE = SLOTS * TB
AUX = 2 * TB
OWN = SLOTS
BF, F32 = jnp.bfloat16, jnp.float32


def lay_out(half, place_ref, piece_ref, scale_ref, *refs):
    outs, sem = refs[:-1], refs[-1]
    copies = []
    for turn in range(SIDE):
        part = lax.rem(place_ref[1 - half] + turn, SIDE)
        first = pl.multiple_of(half * (K // 2) + part * PART, PART)
        copy = pltpu.make_async_copy(
            piece_ref.at[pl.ds(first, PART)], outs[turn].at[:PART], sem.at[turn]
        )
        copy.start()
        copies.append(copy)
    for turn in range(SIDE):
        part = lax.rem(place_ref[1 - half] + turn, SIDE)
        first = half * (K // 2 // QB) + part * PART_SCALES
        first = pl.multiple_of(first, PART_SCALES)
        scale = scale_ref[pl.ds(first, PART_SCALES), :]
        high = scale.astype(BF)
        outs[turn][PART:, :] = jnp.concatenate(
            [high, (scale - high.astype(F32)).astype(BF)], axis=0
        )
    for copy in copies:
        copy.wait()


def laid_out(half, place, pieces, scales):
    shape = jax.ShapeDtypeStruct((PART + 2 * PART_SCALES, COLS), BF)
    return pl.pallas_call(
        functools.partial(lay_out, half),
        in_specs=[
            pl.BlockSpec(memory_space=pltpu.SMEM),
            pl.BlockSpec(memory_space=pltpu.HBM),
            pl.BlockSpec(memory_space=pltpu.VMEM),
        ],
        out_specs=[pl.BlockSpec(memory_space=pltpu.VMEM)] * SIDE,
        out_shape=[shape] * SIDE,
        scratch_shapes=[pltpu.SemaphoreType.DMA((SIDE,))],
        compiler_params=pltpu.CompilerParams(vmem_limit_bytes=32 * 2**20),
        cost_estimate=pl.CostEstimate(
            flops=0, bytes_accessed=2 * K * COLS, transcendentals=0
        ),
    )(place, pieces, scales)


def sum_first(half, place_ref, *refs):
    pieces, outs, scales = refs[:SIDE], refs[SIDE:-1], refs[-1]
    for n, ref in enumerate(pieces):
        both = ref[PART:, :].astype(F32)
        scales[n] = both[:PART_SCALES] + both[PART_SCALES:]
    for turn in range(SIDE):
        part = lax.rem(place_ref[half] + turn, SIDE)
        for block in range(QUARTER // QB):
            row = part * (QUARTER // QB) + block
            first = pl.multiple_of(row * QB, QB)
            total = None
            for n in range(SIDE):
                term = pieces[n][pl.ds(first, QB), :].astype(F32)
                term = term * scales[n, pl.ds(row, 1), :]
                total = term if total is None else total + term
            outs[turn][block * QB : (block + 1) * QB, :] = total


def summed_first(half, place, pieces):
    return pl.pallas_call(
        functools.partial(sum_first, half),
        in_specs=[pl.BlockSpec(memory_space=pltpu.SMEM)]
        + [pl.BlockSpec(memory_space=pltpu.VMEM)] * SIDE,
        out_specs=[pl.BlockSpec(memory_space=pltpu.VMEM)] * SIDE,
        out_shape=[jax.ShapeDtypeStruct((QUARTER, COLS), F32)] * SIDE,
        scratch_shapes=[pltpu.VMEM((SIDE, PART_SCALES, COLS), F32)],
        compiler_params=pltpu.CompilerParams(vmem_limit_bytes=32 * 2**20),
        cost_estimate=pl.CostEstimate(
            flops=K * COLS, bytes_accessed=2 * K * COLS, transcendentals=0
        ),
    )(place, *pieces)


def sum_second(*refs):
    pieces, (high_ref, low_ref) = refs[:SIDE], refs[SIDE:]
    total = pieces[0][...]
    for ref in pieces[1:]:
        total += ref[...]
    high = total.astype(BF)
    high_ref[...] = high
    low_ref[...] = (total - high.astype(F32)).astype(BF)


def summed_second(pieces):
    return pl.pallas_call(
        sum_second,
        in_specs=[pl.BlockSpec(memory_space=pltpu.VMEM)] * SIDE,
        out_specs=[pl.BlockSpec(memory_space=pltpu.VMEM)] * 2,
        out_shape=[jax.ShapeDtypeStruct((QUARTER, COLS), BF)] * 2,
        compiler_params=pltpu.CompilerParams(vmem_limit_bytes=32 * 2**20),
        cost_estimate=pl.CostEstimate(
            flops=4 * SLICE * COLS, bytes_accessed=10 * SLICE * COLS, transcendentals=0
        ),
    )(*pieces)


def tiles(where_ref, *refs):
    (out_ref, dots, squares), refs = refs[-3:], refs[:-3]
    contract = (((0,), (0,)), ((), ()))
    highs, lows, parts = refs[:2], refs[2:4], refs[4:]
    high = [ref[...] for ref in highs]
    low = [ref[...] for ref in lows]
    for n in range(N_EX):
        dot, square = 0.0, 0.0
        for half in range(2):
            part = high[half] if n == 0 else parts[half * (N_EX - 1) + n - 1][...]
            for own in (high[half], low[half]):
                dot += lax.dot_general(own, part, contract, preferred_element_type=F32)
            wide = part.astype(F32)
            square += jnp.sum(wide * wide, axis=0, keepdims=True)
        for half in range(BLK_DEV):
            cut = slice(half * TB, (half + 1) * TB)
            dots[n * BLK_DEV + half] = dot[:, cut]
            squares[n * BLK_DEV + half] = jnp.broadcast_to(square[:, cut], (8, TB))
    own = 0.0
    for half in range(2):
        exact = high[half].astype(F32) + low[half].astype(F32)
        own += jnp.sum(exact * exact, axis=0, keepdims=True)
    for b in range(BLK_DEV):
        rows = slice(b * TB, (b + 1) * TB)
        aux = []
        for s in range(SLOTS):
            at = where_ref[b * SLOTS + s]
            out_ref[rows, s * TB : (s + 1) * TB] = dots[at, rows, :].astype(BF)
            aux.append(squares[at][:1])
        aux.append(own[:, rows])
        aux.append(jnp.zeros((ROWS - SLOTS - 1, TB), F32))
        aux = jnp.concatenate(aux, axis=0)
        first = aux.astype(BF)
        second = (aux - first.astype(F32)).astype(BF)
        both = jnp.concatenate([first, second], axis=1)
        for i in range(TB // ROWS):
            out_ref[b * TB + i * ROWS : b * TB + (i + 1) * ROWS, WIDE:] = both


def partial_tiles(where, highs, lows, parts):
    return pl.pallas_call(
        tiles,
        in_specs=[pl.BlockSpec(memory_space=pltpu.SMEM)]
        + [pl.BlockSpec(memory_space=pltpu.VMEM)] * (4 + len(parts)),
        out_specs=pl.BlockSpec(memory_space=pltpu.VMEM),
        out_shape=jax.ShapeDtypeStruct((COLS, WIDE + AUX), BF),
        scratch_shapes=[
            pltpu.VMEM((N_EX * BLK_DEV, COLS, TB), F32),
            pltpu.VMEM((N_EX * BLK_DEV, 8, TB), F32),
        ],
        compiler_params=pltpu.CompilerParams(vmem_limit_bytes=32 * 2**20),
        cost_estimate=pl.CostEstimate(
            flops=4 * SLICE * COLS * COLS * N_EX,
            bytes_accessed=2 * SLICE * COLS * 9 + 2 * COLS * (WIDE + AUX),
            transcendentals=0,
        ),
    )(where, *highs, *lows, *parts)


def finish(me_ref, sums_ref, out_ref):
    total = sums_ref[0].astype(F32)
    for layer in range(1, LAYERS):
        total += sums_ref[layer].astype(F32)
    squares = total[:, WIDE : WIDE + TB] + total[:, WIDE + TB :]
    inverse = lax.rsqrt(squares / K + 1e-06)
    first = lax.rem(me_ref[0], TB // ROWS) * ROWS
    lane = lax.broadcasted_iota(jnp.int32, (ROWS, TB), 1)
    row = lax.broadcasted_iota(jnp.int32, (ROWS, TB), 0)
    own = jnp.broadcast_to(inverse[OWN : OWN + 1], (ROWS, TB))
    left = jnp.sum(jnp.where(lane == first + row, own, 0.0), axis=1, keepdims=True)
    left = left / math.sqrt(K)
    for s in range(SLOTS):
        cut = slice(s * TB, (s + 1) * TB)
        value = (total[:, cut] * left * inverse[s : s + 1]).astype(BF)
        for layer in range(LAYERS):
            out_ref[layer, :, cut] = value


def finished_rows(me, sums):
    return pl.pallas_call(
        finish,
        in_specs=[
            pl.BlockSpec(memory_space=pltpu.SMEM),
            pl.BlockSpec(memory_space=pltpu.VMEM),
        ],
        out_specs=pl.BlockSpec(memory_space=pltpu.VMEM),
        out_shape=jax.ShapeDtypeStruct((LAYERS, ROWS, WIDE), BF),
        compiler_params=pltpu.CompilerParams(vmem_limit_bytes=32 * 2**20),
        cost_estimate=pl.CostEstimate(
            flops=LAYERS * ROWS * WIDE,
            bytes_accessed=4 * LAYERS * ROWS * WIDE,
            transcendentals=ROWS * TB,
        ),
    )(me, sums)


def partner_places(pairs, ex):
    own = ex * BLK_DEV + jnp.arange(BLK_DEV, dtype=jnp.int32)[:, None, None]
    grouped = pairs.reshape(1, SLOTS, -1, 3)
    row, col = grouped[..., 0], grouped[..., 1]
    partner = jnp.sum(
        jnp.where(row == own, col, 0) + jnp.where(col == own, row, 0), axis=2
    )
    holder, half = partner // BLK_DEV, partner % BLK_DEV
    turn = (ex // 2 - holder // 2) % (N_EX // 2)
    other = (holder % 2) != (ex % 2)
    part = turn + jnp.where(other, N_EX // 2, 0)
    return (part * BLK_DEV + half).reshape(-1).astype(jnp.int32)


def on_device(partials, scales, pairs):
    ex = lax.axis_index("ex")
    layer = lax.axis_index("layer").astype(jnp.int32)
    here = layer.reshape(1)
    place = jnp.stack([layer // SIDE, layer % SIDE])
    where = partner_places(pairs, ex)

    def along(axis, a, turn):
        go = lambda y, x: ((y + turn) % SIDE, x) if axis == 0 else (y, (x + turn) % SIDE)
        to = [go(n // SIDE, n % SIDE) for n in range(LAYERS)]
        return lax.ppermute(a, "layer", [(n, y * SIDE + x) for n, (y, x) in enumerate(to)])

    def exchanged(parts, axis):
        return [parts[0]] + [along(axis, parts[turn], turn) for turn in range(1, SIDE)]

    around = lambda a, d: lax.ppermute(
        a, "ex", [(e, (e + 2 * d) % N_EX) for e in range(N_EX)]
    )
    swap = lambda a: lax.ppermute(a, "ex", [(e, e ^ 1) for e in range(N_EX)])

    highs, lows, others = [], [], []
    for half in range(2):
        parts = laid_out(half, place, partials[0], scales[0])
        parts = summed_first(half, place, exchanged(parts, 1 - half))
        high, low = summed_second(exchanged(parts, half))
        same = [around(high, d) for d in (1, 2, 3)]
        highs.append(high)
        lows.append(low)
        others += [*same, *(swap(a) for a in (high, *same))]
    sums = partial_tiles(where, highs, lows, others)

    across = lambda a: lax.all_to_all(a, "layer", 0, 0, tiled=True)
    sums = across(sums.reshape(LAYERS, ROWS, WIDE + AUX))
    rows = across(finished_rows(here, sums))
    return rows.reshape(COLS, WIDE).astype(F32)


def solution(mesh):
    in_specs = (P("layer", None, "ex"), P("layer", None, "ex"), P())
    out_specs = P("ex", None)
    return jax.shard_map(
        on_device, mesh=mesh, in_specs=in_specs, out_specs=out_specs, check_vma=False
    )
```

```python
import functools
import math

import jax
import jax.numpy as jnp
from jax import lax
from jax.experimental import pallas as pl
from jax.experimental.pallas import tpu as pltpu
from jax.sharding import PartitionSpec as P

K = 8192
TB = 128
QB = 64
SLOTS = 10
LAYERS = 16
N_EX = 8
BLK_DEV = 2
COLS = BLK_DEV * TB
SLICE = K // LAYERS
SIDE = 4
PART = K // 2 // SIDE
PART_SCALES = PART // QB
QUARTER = PART // SIDE
ROWS = COLS // LAYERS
WIDE = SLOTS * TB
AUX = 2 * TB
OWN = SLOTS
BF, F32 = jnp.bfloat16, jnp.float32


def lay_out(half, place_ref, piece_ref, scale_ref, *refs):
    outs, (scales, sem, scale_sem) = refs[:-3], refs[-3:]
    copies, scale_copies = [], []
    for turn in range(SIDE):
        part = lax.rem(place_ref[1 - half] + turn, SIDE)
        first = half * (K // 2 // QB) + part * PART_SCALES
        first = pl.multiple_of(first, PART_SCALES)
        copy = pltpu.make_async_copy(
            scale_ref.at[pl.ds(first, PART_SCALES)], scales.at[turn], scale_sem.at[turn]
        )
        copy.start()
        scale_copies.append(copy)
    for turn in range(SIDE):
        part = lax.rem(place_ref[1 - half] + turn, SIDE)
        first = pl.multiple_of(half * (K // 2) + part * PART, PART)
        copy = pltpu.make_async_copy(
            piece_ref.at[pl.ds(first, PART)], outs[turn].at[:PART], sem.at[turn]
        )
        copy.start()
        copies.append(copy)
    for turn in range(SIDE):
        scale_copies[turn].wait()
        scale = scales[turn]
        high = scale.astype(BF)
        outs[turn][PART:, :] = jnp.concatenate(
            [high, (scale - high.astype(F32)).astype(BF)], axis=0
        )
    for copy in copies:
        copy.wait()


def laid_out(half, place, pieces, scales):
    shape = jax.ShapeDtypeStruct((PART + 2 * PART_SCALES, COLS), BF)
    return pl.pallas_call(
        functools.partial(lay_out, half),
        in_specs=[
            pl.BlockSpec(memory_space=pltpu.SMEM),
            pl.BlockSpec(memory_space=pltpu.HBM),
            pl.BlockSpec(memory_space=pltpu.HBM),
        ],
        out_specs=[pl.BlockSpec(memory_space=pltpu.VMEM)] * SIDE,
        out_shape=[shape] * SIDE,
        scratch_shapes=[
            pltpu.VMEM((SIDE, PART_SCALES, COLS), F32),
            pltpu.SemaphoreType.DMA((SIDE,)),
            pltpu.SemaphoreType.DMA((SIDE,)),
        ],
        compiler_params=pltpu.CompilerParams(vmem_limit_bytes=48 * 2**20),
        cost_estimate=pl.CostEstimate(
            flops=0, bytes_accessed=2 * K * COLS, transcendentals=0
        ),
    )(place, pieces, scales)


def sum_first(half, place_ref, *refs):
    pieces, outs, scales = refs[:SIDE], refs[SIDE:-1], refs[-1]
    for n, ref in enumerate(pieces):
        both = ref[PART:, :].astype(F32)
        scales[n] = both[:PART_SCALES] + both[PART_SCALES:]
    for turn in range(SIDE):
        part = lax.rem(place_ref[half] + turn, SIDE)
        for block in range(QUARTER // QB):
            row = part * (QUARTER // QB) + block
            first = pl.multiple_of(row * QB, QB)
            total = None
            for n in range(SIDE):
                term = pieces[n][pl.ds(first, QB), :].astype(F32)
                term = term * scales[n, pl.ds(row, 1), :]
                total = term if total is None else total + term
            outs[turn][block * QB : (block + 1) * QB, :] = total


def summed_first(half, place, pieces):
    return pl.pallas_call(
        functools.partial(sum_first, half),
        in_specs=[pl.BlockSpec(memory_space=pltpu.SMEM)]
        + [pl.BlockSpec(memory_space=pltpu.VMEM)] * SIDE,
        out_specs=[pl.BlockSpec(memory_space=pltpu.VMEM)] * SIDE,
        out_shape=[jax.ShapeDtypeStruct((QUARTER, COLS), F32)] * SIDE,
        scratch_shapes=[pltpu.VMEM((SIDE, PART_SCALES, COLS), F32)],
        compiler_params=pltpu.CompilerParams(vmem_limit_bytes=32 * 2**20),
        cost_estimate=pl.CostEstimate(
            flops=K * COLS, bytes_accessed=2 * K * COLS, transcendentals=0
        ),
    )(place, *pieces)


def sum_second(*refs):
    pieces, (high_ref, low_ref) = refs[:SIDE], refs[SIDE:]
    total = pieces[0][...]
    for ref in pieces[1:]:
        total += ref[...]
    high = total.astype(BF)
    high_ref[...] = high
    low_ref[...] = (total - high.astype(F32)).astype(BF)


def summed_second(pieces):
    return pl.pallas_call(
        sum_second,
        in_specs=[pl.BlockSpec(memory_space=pltpu.VMEM)] * SIDE,
        out_specs=[pl.BlockSpec(memory_space=pltpu.VMEM)] * 2,
        out_shape=[jax.ShapeDtypeStruct((QUARTER, COLS), BF)] * 2,
        compiler_params=pltpu.CompilerParams(vmem_limit_bytes=32 * 2**20),
        cost_estimate=pl.CostEstimate(
            flops=4 * SLICE * COLS, bytes_accessed=10 * SLICE * COLS, transcendentals=0
        ),
    )(*pieces)


def stacked(parts):
    rows = parts[0].shape[0]

    def stack(*refs):
        for n, ref in enumerate(refs[:-1]):
            refs[-1][n * rows : (n + 1) * rows, :] = ref[...]

    return pl.pallas_call(
        stack,
        in_specs=[pl.BlockSpec(memory_space=pltpu.VMEM)] * len(parts),
        out_specs=pl.BlockSpec(memory_space=pltpu.VMEM),
        out_shape=jax.ShapeDtypeStruct((len(parts) * rows, COLS), BF),
        compiler_params=pltpu.CompilerParams(vmem_limit_bytes=32 * 2**20),
        cost_estimate=pl.CostEstimate(
            flops=0, bytes_accessed=4 * len(parts) * rows * COLS, transcendentals=0
        ),
    )(*parts)


def half_dots(refs, keep):
    high, low = refs[0][...], refs[1][...]
    contract = (((0,), (0,)), ((), ()))
    n = 0
    for ref in (refs[0], *refs[2:]):
        for first in range(0, ref.shape[0], QUARTER):
            part = ref[first : first + QUARTER, :]
            dot = lax.dot_general(high, part, contract, preferred_element_type=F32)
            dot += lax.dot_general(low, part, contract, preferred_element_type=F32)
            wide = part.astype(F32)
            keep(n, dot, jnp.sum(wide * wide, axis=0, keepdims=True))
            n += 1
    exact = high.astype(F32) + low.astype(F32)
    return jnp.sum(exact * exact, axis=0, keepdims=True)


def first_tiles(*refs):
    refs, (dots, squares) = refs[:-2], refs[-2:]

    def keep(n, dot, square):
        for b in range(BLK_DEV):
            dots[n * BLK_DEV + b] = dot[:, b * TB : (b + 1) * TB]
        squares[n : n + 1, :] = square

    own = half_dots(refs, keep)
    squares[N_EX:, :] = jnp.broadcast_to(own, (N_EX, COLS))


def first_dots(parts):
    return pl.pallas_call(
        first_tiles,
        in_specs=[pl.BlockSpec(memory_space=pltpu.VMEM)] * len(parts),
        out_specs=[pl.BlockSpec(memory_space=pltpu.VMEM)] * 2,
        out_shape=[
            jax.ShapeDtypeStruct((N_EX * BLK_DEV, COLS, TB), F32),
            jax.ShapeDtypeStruct((2 * N_EX, COLS), F32),
        ],
        compiler_params=pltpu.CompilerParams(vmem_limit_bytes=32 * 2**20),
        cost_estimate=pl.CostEstimate(
            flops=2 * SLICE * COLS * COLS * N_EX,
            bytes_accessed=SLICE * COLS * 9 + 4 * N_EX * COLS * COLS,
            transcendentals=0,
        ),
    )(*parts)


def tiles(where_ref, dots_ref, squares_ref, *refs):
    refs, (out_ref, dots, squares) = refs[:-3], refs[-3:]

    def keep(n, dot, square):
        square += squares_ref[n : n + 1, :]
        for b in range(BLK_DEV):
            cut = slice(b * TB, (b + 1) * TB)
            dots[n * BLK_DEV + b] = dot[:, cut] + dots_ref[n * BLK_DEV + b]
            squares[n * BLK_DEV + b] = jnp.broadcast_to(square[:, cut], (8, TB))

    own = half_dots(refs, keep) + squares_ref[N_EX : N_EX + 1, :]
    for b in range(BLK_DEV):
        rows = slice(b * TB, (b + 1) * TB)
        aux = []
        for s in range(SLOTS):
            at = where_ref[b * SLOTS + s]
            out_ref[rows, s * TB : (s + 1) * TB] = dots[at, rows, :].astype(BF)
            aux.append(squares[at][:1])
        aux.append(own[:, rows])
        aux.append(jnp.zeros((ROWS - SLOTS - 1, TB), F32))
        aux = jnp.concatenate(aux, axis=0)
        first = aux.astype(BF)
        second = (aux - first.astype(F32)).astype(BF)
        both = jnp.concatenate([first, second], axis=1)
        for i in range(TB // ROWS):
            out_ref[b * TB + i * ROWS : b * TB + (i + 1) * ROWS, WIDE:] = both


def partial_tiles(where, dots, squares, parts):
    return pl.pallas_call(
        tiles,
        in_specs=[pl.BlockSpec(memory_space=pltpu.SMEM)]
        + [pl.BlockSpec(memory_space=pltpu.VMEM)] * (2 + len(parts)),
        out_specs=pl.BlockSpec(memory_space=pltpu.VMEM),
        out_shape=jax.ShapeDtypeStruct((COLS, WIDE + AUX), BF),
        scratch_shapes=[
            pltpu.VMEM((N_EX * BLK_DEV, COLS, TB), F32),
            pltpu.VMEM((N_EX * BLK_DEV, 8, TB), F32),
        ],
        compiler_params=pltpu.CompilerParams(vmem_limit_bytes=32 * 2**20),
        cost_estimate=pl.CostEstimate(
            flops=2 * SLICE * COLS * COLS * N_EX,
            bytes_accessed=SLICE * COLS * 9 + 4 * N_EX * COLS * COLS,
            transcendentals=0,
        ),
    )(where, dots, squares, *parts)


def finish(me_ref, sums_ref, out_ref):
    total = sums_ref[0].astype(F32)
    for layer in range(1, LAYERS):
        total += sums_ref[layer].astype(F32)
    squares = total[:, WIDE : WIDE + TB] + total[:, WIDE + TB :]
    inverse = lax.rsqrt(squares / K + 1e-06)
    first = lax.rem(me_ref[0], TB // ROWS) * ROWS
    lane = lax.broadcasted_iota(jnp.int32, (ROWS, TB), 1)
    row = lax.broadcasted_iota(jnp.int32, (ROWS, TB), 0)
    own = jnp.broadcast_to(inverse[OWN : OWN + 1], (ROWS, TB))
    left = jnp.sum(jnp.where(lane == first + row, own, 0.0), axis=1, keepdims=True)
    left = left / math.sqrt(K)
    for s in range(SLOTS):
        cut = slice(s * TB, (s + 1) * TB)
        value = (total[:, cut] * left * inverse[s : s + 1]).astype(BF)
        for layer in range(LAYERS):
            out_ref[layer, :, cut] = value


def finished_rows(me, sums):
    return pl.pallas_call(
        finish,
        in_specs=[
            pl.BlockSpec(memory_space=pltpu.SMEM),
            pl.BlockSpec(memory_space=pltpu.VMEM),
        ],
        out_specs=pl.BlockSpec(memory_space=pltpu.VMEM),
        out_shape=jax.ShapeDtypeStruct((LAYERS, ROWS, WIDE), BF),
        compiler_params=pltpu.CompilerParams(vmem_limit_bytes=32 * 2**20),
        cost_estimate=pl.CostEstimate(
            flops=LAYERS * ROWS * WIDE,
            bytes_accessed=4 * LAYERS * ROWS * WIDE,
            transcendentals=ROWS * TB,
        ),
    )(me, sums)


def partner_places(pairs, ex):
    own = ex * BLK_DEV + jnp.arange(BLK_DEV, dtype=jnp.int32)[:, None, None]
    grouped = pairs.reshape(1, SLOTS, -1, 3)
    row, col = grouped[..., 0], grouped[..., 1]
    partner = jnp.sum(
        jnp.where(row == own, col, 0) + jnp.where(col == own, row, 0), axis=2
    )
    holder, half = partner // BLK_DEV, partner % BLK_DEV
    turn = (ex // 2 - holder // 2) % (N_EX // 2)
    other = (holder % 2) != (ex % 2)
    part = turn ^ (turn >> 1)
    part = part + jnp.where(other, N_EX // 2, 0)
    return (part * BLK_DEV + half).reshape(-1).astype(jnp.int32)


def on_device(partials, scales, pairs):
    ex = lax.axis_index("ex")
    layer = lax.axis_index("layer").astype(jnp.int32)
    here = layer.reshape(1)
    place = jnp.stack([layer // SIDE, layer % SIDE])
    where = partner_places(pairs, ex)

    def along(axis, a, turn):
        go = lambda y, x: ((y + turn) % SIDE, x) if axis == 0 else (y, (x + turn) % SIDE)
        to = [go(n // SIDE, n % SIDE) for n in range(LAYERS)]
        return lax.ppermute(a, "layer", [(n, y * SIDE + x) for n, (y, x) in enumerate(to)])

    def exchanged(parts, axis):
        return [parts[0]] + [along(axis, parts[turn], turn) for turn in range(1, SIDE)]

    around = lambda a, d: lax.ppermute(
        a, "ex", [(e, (e + 2 * d) % N_EX) for e in range(N_EX)]
    )
    swap = lambda a: lax.ppermute(a, "ex", [(e, e ^ 1) for e in range(N_EX)])

    parts = []
    for half in range(2):
        pieces = laid_out(half, place, partials[0], scales[0])
        pieces = summed_first(half, place, exchanged(pieces, 1 - half))
        high, low = summed_second(exchanged(pieces, half))
        right, left = around(high, 1), around(high, -1)
        if half == 0:
            far = around(right, 1)
            swapped = [swap(stacked([high, right, left, far]))]
        else:
            near = swap(stacked([high, right, left]))
            far = around(left, -1)
            swapped = [near, swap(far)]
        parts.append([high, low, right, left, far, *swapped])
    dots, squares = first_dots(parts[0])
    sums = partial_tiles(where, dots, squares, parts[1])

    across = lambda a: lax.all_to_all(a, "layer", 0, 0, tiled=True)
    sums = across(sums.reshape(LAYERS, ROWS, WIDE + AUX))
    rows = across(finished_rows(here, sums))
    return rows.reshape(COLS, WIDE).astype(F32)


def solution(mesh):
    in_specs = (P("layer", None, "ex"), P("layer", None, "ex"), P())
    out_specs = P("ex", None)
    return jax.shard_map(
        on_device, mesh=mesh, in_specs=in_specs, out_specs=out_specs, check_vma=False
    )
```

```python
import functools
import math

import jax
import jax.numpy as jnp
from jax import lax
from jax.experimental import pallas as pl
from jax.experimental.pallas import tpu as pltpu
from jax.sharding import PartitionSpec as P

K = 8192
TB = 128
QB = 64
SLOTS = 10
LAYERS = 16
N_EX = 8
BLK_DEV = 2
COLS = BLK_DEV * TB
SLICE = K // LAYERS
SIDE = 4
PART = K // 2 // SIDE
PART_SCALES = PART // QB
QUARTER = PART // SIDE
ROWS = COLS // LAYERS
WIDE = SLOTS * TB
AUX = 2 * TB
OWN = SLOTS
BF, F32 = jnp.bfloat16, jnp.float32


def lay_out(half, place_ref, piece_ref, scale_ref, *refs):
    outs, sem = refs[:-1], refs[-1]
    copies = []
    for turn in range(SIDE):
        part = lax.rem(place_ref[1 - half] + turn, SIDE)
        first = pl.multiple_of(half * (K // 2) + part * PART, PART)
        copy = pltpu.make_async_copy(
            piece_ref.at[pl.ds(first, PART)], outs[turn].at[:PART], sem.at[turn]
        )
        copy.start()
        copies.append(copy)
    for turn in range(SIDE):
        part = lax.rem(place_ref[1 - half] + turn, SIDE)
        first = half * (K // 2 // QB) + part * PART_SCALES
        first = pl.multiple_of(first, PART_SCALES)
        scale = scale_ref[pl.ds(first, PART_SCALES), :]
        high = scale.astype(BF)
        outs[turn][PART:, :] = jnp.concatenate(
            [high, (scale - high.astype(F32)).astype(BF)], axis=0
        )
    for copy in copies:
        copy.wait()


def laid_out(half, place, pieces, scales):
    shape = jax.ShapeDtypeStruct((PART + 2 * PART_SCALES, COLS), BF)
    return pl.pallas_call(
        functools.partial(lay_out, half),
        in_specs=[
            pl.BlockSpec(memory_space=pltpu.SMEM),
            pl.BlockSpec(memory_space=pltpu.HBM),
            pl.BlockSpec(memory_space=pltpu.VMEM),
        ],
        out_specs=[pl.BlockSpec(memory_space=pltpu.VMEM)] * SIDE,
        out_shape=[shape] * SIDE,
        scratch_shapes=[pltpu.SemaphoreType.DMA((SIDE,))],
        compiler_params=pltpu.CompilerParams(vmem_limit_bytes=32 * 2**20),
        cost_estimate=pl.CostEstimate(
            flops=0, bytes_accessed=2 * K * COLS, transcendentals=0
        ),
    )(place, pieces, scales)


def sum_first(half, place_ref, *refs):
    pieces, outs, scales = refs[:SIDE], refs[SIDE:-1], refs[-1]
    for n, ref in enumerate(pieces):
        both = ref[PART:, :].astype(F32)
        scales[n] = both[:PART_SCALES] + both[PART_SCALES:]
    for turn in range(SIDE):
        part = lax.rem(place_ref[half] + turn, SIDE)
        for block in range(QUARTER // QB):
            row = part * (QUARTER // QB) + block
            first = pl.multiple_of(row * QB, QB)
            total = None
            for n in range(SIDE):
                term = pieces[n][pl.ds(first, QB), :].astype(F32)
                term = term * scales[n, pl.ds(row, 1), :]
                total = term if total is None else total + term
            outs[turn][block * QB : (block + 1) * QB, :] = total


def summed_first(half, place, pieces):
    return pl.pallas_call(
        functools.partial(sum_first, half),
        in_specs=[pl.BlockSpec(memory_space=pltpu.SMEM)]
        + [pl.BlockSpec(memory_space=pltpu.VMEM)] * SIDE,
        out_specs=[pl.BlockSpec(memory_space=pltpu.VMEM)] * SIDE,
        out_shape=[jax.ShapeDtypeStruct((QUARTER, COLS), F32)] * SIDE,
        scratch_shapes=[pltpu.VMEM((SIDE, PART_SCALES, COLS), F32)],
        compiler_params=pltpu.CompilerParams(vmem_limit_bytes=32 * 2**20),
        cost_estimate=pl.CostEstimate(
            flops=K * COLS, bytes_accessed=2 * K * COLS, transcendentals=0
        ),
    )(place, *pieces)


def sum_second(*refs):
    pieces, (high_ref, low_ref) = refs[:SIDE], refs[SIDE:]
    total = pieces[0][...]
    for ref in pieces[1:]:
        total += ref[...]
    high = total.astype(BF)
    high_ref[...] = high
    low_ref[...] = (total - high.astype(F32)).astype(BF)


def summed_second(pieces):
    return pl.pallas_call(
        sum_second,
        in_specs=[pl.BlockSpec(memory_space=pltpu.VMEM)] * SIDE,
        out_specs=[pl.BlockSpec(memory_space=pltpu.VMEM)] * 2,
        out_shape=[jax.ShapeDtypeStruct((QUARTER, COLS), BF)] * 2,
        compiler_params=pltpu.CompilerParams(vmem_limit_bytes=32 * 2**20),
        cost_estimate=pl.CostEstimate(
            flops=4 * SLICE * COLS, bytes_accessed=10 * SLICE * COLS, transcendentals=0
        ),
    )(*pieces)


def stacked(parts):
    rows = parts[0].shape[0]

    def stack(*refs):
        for n, ref in enumerate(refs[:-1]):
            refs[-1][n * rows : (n + 1) * rows, :] = ref[...]

    return pl.pallas_call(
        stack,
        in_specs=[pl.BlockSpec(memory_space=pltpu.VMEM)] * len(parts),
        out_specs=pl.BlockSpec(memory_space=pltpu.VMEM),
        out_shape=jax.ShapeDtypeStruct((len(parts) * rows, COLS), BF),
        compiler_params=pltpu.CompilerParams(vmem_limit_bytes=32 * 2**20),
        cost_estimate=pl.CostEstimate(
            flops=0, bytes_accessed=4 * len(parts) * rows * COLS, transcendentals=0
        ),
    )(*parts)


def tiles(where_ref, *refs):
    (out_ref, dots, squares), refs = refs[-3:], refs[:-3]
    highs, lows, parts = refs[:2], refs[2:4], refs[4:]
    high = [ref[...] for ref in highs]
    low = [ref[...] for ref in lows]
    turned = [(high[half].T, low[half].T) for half in range(2)]
    for n in range(N_EX):
        dot, square = 0.0, 0.0
        for half in range(2):
            *same, swapped = parts[half * SIDE : (half + 1) * SIDE]
            if n == 0:
                part = high[half]
            elif n < SIDE:
                part = same[n - 1][...]
            else:
                part = swapped[(n - SIDE) * QUARTER : (n - SIDE + 1) * QUARTER, :]
            for own in turned[half]:
                dot += jnp.dot(own, part, preferred_element_type=F32)
            wide = part.astype(F32)
            square += jnp.sum(wide * wide, axis=0, keepdims=True)
        for half in range(BLK_DEV):
            cut = slice(half * TB, (half + 1) * TB)
            dots[n * BLK_DEV + half] = dot[:, cut]
            squares[n * BLK_DEV + half] = jnp.broadcast_to(square[:, cut], (8, TB))
    own = 0.0
    for half in range(2):
        exact = high[half].astype(F32) + low[half].astype(F32)
        own += jnp.sum(exact * exact, axis=0, keepdims=True)
    for b in range(BLK_DEV):
        rows = slice(b * TB, (b + 1) * TB)
        aux = []
        for s in range(SLOTS):
            at = where_ref[b * SLOTS + s]
            out_ref[rows, s * TB : (s + 1) * TB] = dots[at, rows, :].astype(BF)
            aux.append(squares[at][:1])
        aux.append(own[:, rows])
        aux.append(jnp.zeros((ROWS - SLOTS - 1, TB), F32))
        aux = jnp.concatenate(aux, axis=0)
        first = aux.astype(BF)
        second = (aux - first.astype(F32)).astype(BF)
        both = jnp.concatenate([first, second], axis=1)
        for i in range(TB // ROWS):
            out_ref[b * TB + i * ROWS : b * TB + (i + 1) * ROWS, WIDE:] = both


def partial_tiles(where, highs, lows, parts):
    return pl.pallas_call(
        tiles,
        in_specs=[pl.BlockSpec(memory_space=pltpu.SMEM)]
        + [pl.BlockSpec(memory_space=pltpu.VMEM)] * (4 + len(parts)),
        out_specs=pl.BlockSpec(memory_space=pltpu.VMEM),
        out_shape=jax.ShapeDtypeStruct((COLS, WIDE + AUX), BF),
        scratch_shapes=[
            pltpu.VMEM((N_EX * BLK_DEV, COLS, TB), F32),
            pltpu.VMEM((N_EX * BLK_DEV, 8, TB), F32),
        ],
        compiler_params=pltpu.CompilerParams(vmem_limit_bytes=32 * 2**20),
        cost_estimate=pl.CostEstimate(
            flops=4 * SLICE * COLS * COLS * N_EX,
            bytes_accessed=2 * SLICE * COLS * 9 + 2 * COLS * (WIDE + AUX),
            transcendentals=0,
        ),
    )(where, *highs, *lows, *parts)


def finish(me_ref, sums_ref, out_ref):
    total = sums_ref[0].astype(F32)
    for layer in range(1, LAYERS):
        total += sums_ref[layer].astype(F32)
    squares = total[:, WIDE : WIDE + TB] + total[:, WIDE + TB :]
    inverse = lax.rsqrt(squares / K + 1e-06)
    first = lax.rem(me_ref[0], TB // ROWS) * ROWS
    lane = lax.broadcasted_iota(jnp.int32, (ROWS, TB), 1)
    row = lax.broadcasted_iota(jnp.int32, (ROWS, TB), 0)
    own = jnp.broadcast_to(inverse[OWN : OWN + 1], (ROWS, TB))
    left = jnp.sum(jnp.where(lane == first + row, own, 0.0), axis=1, keepdims=True)
    left = left / math.sqrt(K)
    for s in range(SLOTS):
        cut = slice(s * TB, (s + 1) * TB)
        value = (total[:, cut] * left * inverse[s : s + 1]).astype(BF)
        for layer in range(LAYERS):
            out_ref[layer, :, cut] = value


def finished_rows(me, sums):
    return pl.pallas_call(
        finish,
        in_specs=[
            pl.BlockSpec(memory_space=pltpu.SMEM),
            pl.BlockSpec(memory_space=pltpu.VMEM),
        ],
        out_specs=pl.BlockSpec(memory_space=pltpu.VMEM),
        out_shape=jax.ShapeDtypeStruct((LAYERS, ROWS, WIDE), BF),
        compiler_params=pltpu.CompilerParams(vmem_limit_bytes=32 * 2**20),
        cost_estimate=pl.CostEstimate(
            flops=LAYERS * ROWS * WIDE,
            bytes_accessed=4 * LAYERS * ROWS * WIDE,
            transcendentals=ROWS * TB,
        ),
    )(me, sums)


def partner_places(pairs, ex):
    own = ex * BLK_DEV + jnp.arange(BLK_DEV, dtype=jnp.int32)[:, None, None]
    grouped = pairs.reshape(1, SLOTS, -1, 3)
    row, col = grouped[..., 0], grouped[..., 1]
    partner = jnp.sum(
        jnp.where(row == own, col, 0) + jnp.where(col == own, row, 0), axis=2
    )
    holder, half = partner // BLK_DEV, partner % BLK_DEV
    turn = (ex // 2 - holder // 2) % (N_EX // 2)
    other = (holder % 2) != (ex % 2)
    part = turn + jnp.where(other, N_EX // 2, 0)
    return (part * BLK_DEV + half).reshape(-1).astype(jnp.int32)


def on_device(partials, scales, pairs):
    ex = lax.axis_index("ex")
    layer = lax.axis_index("layer").astype(jnp.int32)
    here = layer.reshape(1)
    place = jnp.stack([layer // SIDE, layer % SIDE])
    where = partner_places(pairs, ex)

    def along(axis, a, turn):
        go = lambda y, x: ((y + turn) % SIDE, x) if axis == 0 else (y, (x + turn) % SIDE)
        to = [go(n // SIDE, n % SIDE) for n in range(LAYERS)]
        return lax.ppermute(a, "layer", [(n, y * SIDE + x) for n, (y, x) in enumerate(to)])

    def exchanged(parts, axis):
        return [parts[0]] + [along(axis, parts[turn], turn) for turn in range(1, SIDE)]

    around = lambda a, d: lax.ppermute(
        a, "ex", [(e, (e + 2 * d) % N_EX) for e in range(N_EX)]
    )
    swap = lambda a: lax.ppermute(a, "ex", [(e, e ^ 1) for e in range(N_EX)])

    highs, lows, others = [], [], []
    for half in range(2):
        parts = laid_out(half, place, partials[0], scales[0])
        parts = summed_first(half, place, exchanged(parts, 1 - half))
        high, low = summed_second(exchanged(parts, half))
        same = [around(high, d) for d in (1, 2, 3)]
        highs.append(high)
        lows.append(low)
        others += [*same, swap(stacked([high, *same]))]
    sums = partial_tiles(where, highs, lows, others)

    across = lambda a: lax.all_to_all(a, "layer", 0, 0, tiled=True)
    sums = across(sums.reshape(LAYERS, ROWS, WIDE + AUX))
    rows = across(finished_rows(here, sums))
    return rows.reshape(COLS, WIDE).astype(F32)


def solution(mesh):
    in_specs = (P("layer", None, "ex"), P("layer", None, "ex"), P())
    out_specs = P("ex", None)
    return jax.shard_map(
        on_device, mesh=mesh, in_specs=in_specs, out_specs=out_specs, check_vma=False
    )
```
